32 devices in a mesh: dp: 8 (over y, x, core), replica: 4 (over z).
Axes of the slice: x: 2, y: 2, z: 4, core: 2. Of those that a mesh axis runs over, the one named last changes fastest.
Arguments:
- image_emb: bfloat16 [4, 1024, 1152], P('replica', 'dp'), may hold values from -6 to 6
- text_feat: bfloat16 [4, 1024, 1152], P('replica', 'dp'), may hold values from -6 to 6
- head_w: bfloat16 [1152, 1152], replicated, may hold values from -0.1875 to 0.1875
- log_scale: float32 [1], replicated, may hold values from 1.6 to 2.4
- bias: float32 [1], replicated, may hold values from -2 to 0
- pair_ids: int32 [4, 1024], P('replica', 'dp'), may hold values from 0 to 127
Outputs:
- grad_feat: bfloat16 [4, 1024, 1152], P('replica', 'dp')
- head_grad: float32 [1152, 1152], P('replica', 'dp')
The draws below stay inside these ranges and needn't reach their ends.
All inputs are finite; a program needn't handle non-finite values.
Results may differ from the reference program's by a relative error of at most 0.017.
Values may be sent and summed in bfloat16 or wider, within the bound.
No kernel may reach another device: no remote copies, remote signals or barrier semaphores. Data moves between devices by JAX's collectives and lax.ppermute only.
A program may use at most 64 MiB of HBM per device.

```python
import jax
import jax.numpy as jnp
from jax import lax

D = 1152
E = 1152
TOK_DEV = 128
HOPS = 3
TOKENS = 1024
N_DP = 8
N_REPLICA = 4


def place_ends(result, stream_key, smallest, largest):
    extent = result.shape
    spot = [jax.random.randint(jax.random.fold_in(stream_key, axis), (), 0, extent[axis]) for axis in range(len(extent))]
    result = result.at[tuple(spot)].set(smallest)
    longest = extent.index(max(extent))
    spot[longest] = (spot[longest] + 1) % extent[longest]
    return result.at[tuple(spot)].set(largest)


def level_of(stream_key, dims, pieces, low, largest):
    def one(axis_at, blocks):
        steps = jax.random.uniform(jax.random.fold_in(jax.random.fold_in(stream_key, 6), axis_at), (blocks,), jnp.float32, low / len(pieces), largest / len(pieces))
        return jnp.repeat(jnp.exp(steps), dims[axis_at] // blocks).reshape((-1,) + (1,) * (len(dims) - axis_at - 1))

    gain = one(*pieces[0])
    for cut in pieces[1:]:
        gain = gain * one(*cut)
    return gain


def bell_draw(stream_key, dims, deviation, reach, cuts=(), held_as=jnp.bfloat16):
    drawn = deviation * jax.random.normal(stream_key, dims, jnp.float32)
    if cuts:
        drawn = drawn * level_of(stream_key, dims, cuts, -0.22, 0.18)
    return jnp.clip(drawn, -reach, reach).astype(held_as)


def setup_inputs(seed: int = 0) -> dict:
    streams_of = jax.random.split(jax.random.key(seed), 7)
    image_emb = bell_draw(streams_of[0], (N_REPLICA, TOKENS, E), 1.0, 6.0, ((0, 4), (1, 8)))
    text_feat = bell_draw(streams_of[1], (N_REPLICA, TOKENS, D), 1.0, 6.0, ((0, 4), (1, 8)))
    head_w = bell_draw(streams_of[2], (D, E), D ** -0.5, 0.1875)
    log_scale = jnp.clip(jax.random.uniform(streams_of[3], (1,), jnp.float32, 1.6, 2.4), 1.6, 2.4)
    bias = jnp.clip(jax.random.uniform(streams_of[4], (1,), jnp.float32, -2.0, 0.0), -2.0, 0.0)
    pair_ids = place_ends(jax.random.randint(streams_of[5], (N_REPLICA, TOKENS), 0, TOK_DEV), jax.random.fold_in(streams_of[5], 1), 0, TOK_DEV - 1).astype(jnp.int32)
    return {"image_emb": image_emb, "text_feat": text_feat, "head_w": head_w, "log_scale": log_scale, "bias": bias, "pair_ids": pair_ids}


LOSS_SCALE = 2048.0

def group_grads(images, feats, ids, head_w, scale, shift_b):
    blocks = N_DP
    rows = feats.shape[0] // blocks
    width = images.shape[1]
    factor = LOSS_SCALE / (HOPS * rows)
    img32 = images.astype(jnp.float32)
    unit_img = (img32 / jnp.sqrt(lax.optimization_barrier(jnp.sum(img32 * img32, axis=1, keepdims=True)) + 1e-06)).astype(jnp.bfloat16)
    raw = jnp.dot(feats, head_w, preferred_element_type=jnp.float32)
    norms = jnp.sqrt(lax.optimization_barrier(jnp.sum(raw * raw, axis=1, keepdims=True)) + 1e-06)
    unit_txt = raw / norms
    txt_bf = unit_txt.astype(jnp.bfloat16)
    img_blocks = unit_img.astype(jnp.float32).reshape(blocks, rows, width)
    txt_blocks = txt_bf.astype(jnp.float32).reshape(blocks, rows, width)
    id_blocks = ids.reshape(blocks, rows)
    dvec = jnp.zeros((blocks, rows, width), jnp.float32)
    for offset in range(HOPS):
        txt_here = jnp.roll(txt_blocks, offset, axis=0)
        ids_here = jnp.roll(id_blocks, offset, axis=0)
        sims = jnp.einsum('bie,bje->bij', img_blocks, txt_here)
        logits = scale * sims + shift_b
        match = (id_blocks[:, :, None] == ids_here[:, None, :]).astype(jnp.float32)
        grads = (factor * (jax.nn.sigmoid(logits) - match)).astype(jnp.bfloat16).astype(jnp.float32)
        term = jnp.einsum('bij,bie->bje', grads, img_blocks)
        dvec = dvec + jnp.roll(term, -offset, axis=0)
    dvec = scale * dvec.reshape(blocks * rows, width)
    dzed = ((dvec - unit_txt * lax.optimization_barrier(jnp.sum(unit_txt * dvec, axis=1, keepdims=True))) / norms).astype(jnp.bfloat16)
    grad_feat = jnp.dot(dzed, head_w.T, preferred_element_type=jnp.float32).astype(jnp.bfloat16)
    head_term = jnp.dot(feats.T, dzed, preferred_element_type=jnp.float32)
    return (grad_feat, head_term)

def reference(image_emb, text_feat, head_w, log_scale, bias, pair_ids):
    scale = jnp.exp(log_scale[0])
    shift_b = bias[0]

    def one_group(carry, inputs):
        images, feats, ids = inputs
        grad_feat, head_term = group_grads(images, feats, ids, head_w, scale, shift_b)
        return (carry + head_term, grad_feat)
    start = jnp.zeros((head_w.shape[0], head_w.shape[1]), jnp.float32)
    head_grad, grad_feat = lax.scan(one_group, start, (image_emb, text_feat, pair_ids))
    return (grad_feat, head_grad)
```

```python
import jax
import jax.numpy as jnp
from jax import lax
from jax.sharding import PartitionSpec as P

HOPS = 3
LOSS_SCALE = 2048.0


def rotated(x, axis, by):
    size = lax.axis_size(axis)
    return lax.ppermute(x, axis, [(i, (i + by) % size) for i in range(size)])


def swapped(x, axis, mask):
    size = lax.axis_size(axis)
    return lax.ppermute(x, axis, [(i, i ^ mask) for i in range(size)])


def shards(image_emb, text_feat, head_w, log_scale, bias, pair_ids):
    images = image_emb[0]
    feats = text_feat[0]
    ids = pair_ids[0]
    rows = feats.shape[0]
    dp = lax.axis_size("dp")
    replica = lax.axis_size("replica")
    chips = dp // 2
    factor = LOSS_SCALE / (HOPS * rows)
    scale = jnp.exp(log_scale[0])
    shift_b = bias[0]

    others = [rotated(images, "dp", -k) for k in range(1, HOPS)]
    other_ids = [rotated(ids, "dp", -k) for k in range(1, HOPS)]
    held = [feats] + [swapped(feats, "dp", 2 * k) for k in range(1, chips)]
    held2 = [swapped(f, "dp", 1) for f in held]

    raw = jnp.dot(feats, head_w, preferred_element_type=jnp.float32)
    norms = jnp.sqrt(jnp.sum(raw * raw, axis=1, keepdims=True) + 1e-06)
    unit_txt = raw / norms
    txt_bf = unit_txt.astype(jnp.bfloat16)

    imgs = jnp.concatenate([images] + others, axis=0)
    img_ids = jnp.concatenate([ids] + other_ids, axis=0)
    img32 = imgs.astype(jnp.float32)
    unit_img = (img32 / jnp.sqrt(jnp.sum(img32 * img32, axis=1, keepdims=True) + 1e-06)).astype(
        jnp.bfloat16
    )
    sims = lax.dot_general(
        txt_bf, unit_img, (((1,), (1,)), ((), ())), preferred_element_type=jnp.float32
    )
    match = (ids[:, None] == img_ids[None, :]).astype(jnp.float32)
    grads = (factor * (jax.nn.sigmoid(scale * sims + shift_b) - match)).astype(jnp.bfloat16)
    dvec = scale * jnp.dot(grads, unit_img, preferred_element_type=jnp.float32)
    dzed = ((dvec - unit_txt * jnp.sum(unit_txt * dvec, axis=1, keepdims=True)) / norms).astype(
        jnp.bfloat16
    )
    grad_feat = lax.dot_general(
        dzed, head_w, (((1,), (1,)), ((), ())), preferred_element_type=jnp.float32
    ).astype(jnp.bfloat16)

    me = lax.axis_index("dp")
    chip, core = me // 2, me % 2
    cols = head_w.shape[1] // dp
    dz_t = dzed.T
    parts = [
        lax.dynamic_slice_in_dim(dz_t, (chip ^ k) * 2 * cols, 2 * cols, 0) for k in range(chips)
    ]
    got = [parts[0]] + [swapped(parts[k], "dp", 2 * k) for k in range(1, chips)]
    got2 = [swapped(g, "dp", 1) for g in got]
    dz_all = jnp.concatenate(got + got2, axis=1)
    dz_all = lax.dynamic_slice_in_dim(dz_all, core * cols, cols, 0)
    feats_all = jnp.concatenate(held + held2, axis=0)
    local_head = lax.dot_general(
        feats_all, dz_all, (((0,), (1,)), ((), ())), preferred_element_type=jnp.float32
    )
    r = lax.axis_index("replica")
    depth = head_w.shape[0] // replica
    head_grad = lax.dynamic_slice_in_dim(local_head, r * depth, depth, 0)
    local_bf = local_head.astype(jnp.bfloat16)
    for k in range(1, replica):
        piece = lax.dynamic_slice_in_dim(local_bf, (r ^ k) * depth, depth, 0)
        head_grad = head_grad + swapped(piece, "replica", k).astype(jnp.float32)
    return (grad_feat[None], head_grad)


def solution(mesh):
    return jax.shard_map(
        shards,
        mesh=mesh,
        in_specs=(
            P("replica", "dp", None),
            P("replica", "dp", None),
            P(),
            P(),
            P(),
            P("replica", "dp"),
        ),
        out_specs=(P("replica", "dp", None), P("replica", "dp")),
        check_vma=False,
    )
```

```python
import functools

import jax
import jax.numpy as jnp
from jax import lax
from jax.experimental import pallas as pl
from jax.experimental.pallas import tpu as pltpu
from jax.sharding import PartitionSpec as P

HOPS = 3
LOSS_SCALE = 2048.0
LANES = 128
VMEM = pl.BlockSpec(memory_space=pltpu.VMEM)
SMEM = pl.BlockSpec(memory_space=pltpu.SMEM)
NT = (((1,), (1,)), ((), ()))


def grant(mib):
    return pltpu.CompilerParams(vmem_limit_bytes=mib * 2**20)


def rotated(x, axis, by):
    size = lax.axis_size(axis)
    return lax.ppermute(x, axis, [(i, (i + by) % size) for i in range(size)])


def swapped(x, axis, mask):
    size = lax.axis_size(axis)
    return lax.ppermute(x, axis, [(i, i ^ mask) for i in range(size)])


def after(x, first):
    return lax.optimization_barrier((x, first))[0]


def in_order(core, own, other):
    first = jnp.where(core == 0, own, other)
    second = jnp.where(core == 0, other, own)
    return jnp.concatenate([first, second], axis=0)


def pair_term(factor, scale, shift_b, txt_bf, row_ids, images, image_ids, skip):
    wide = images.astype(jnp.float32)
    total = jnp.sum(wide * wide, axis=1, keepdims=True) + 1e-06
    unit_img = (wide * (1.0 / jnp.sqrt(total))).astype(jnp.bfloat16)
    sims = lax.dot_general(txt_bf, unit_img, NT, preferred_element_type=jnp.float32)
    rows = sims.shape[0] // 2
    match = (row_ids == image_ids).astype(jnp.float32)
    grads = factor * (jax.nn.sigmoid(scale * sims + shift_b) - match)
    row = lax.broadcasted_iota(jnp.int32, sims.shape, 0) >= rows
    col = lax.broadcasted_iota(jnp.int32, sims.shape, 1) >= rows
    away = (row == bool(skip[0])) & (col == bool(skip[1]))
    grads = jnp.where(away, 0.0, grads).astype(jnp.bfloat16)
    return jnp.dot(grads, unit_img, preferred_element_type=jnp.float32)


def own_kernel(
    factor, scalars, place, feats, feats2, head_w, img, img2, ids,
    unit_out, inverse_out, ids_out, term_out,
):
    core = place[0]
    both = in_order(core, feats[...], feats2[...])
    text = jnp.dot(both, head_w[...], preferred_element_type=jnp.float32)
    inverse = 1.0 / jnp.sqrt(jnp.sum(text * text, axis=1, keepdims=True) + 1e-06)
    unit_txt = text * inverse
    unit_out[...] = unit_txt
    rows = text.shape[0]
    inverse_out[...] = jnp.broadcast_to(inverse, (rows, LANES))
    chip_ids = jnp.concatenate([ids[:1, :], ids[1:2, :]], axis=1)
    row_ids = jnp.broadcast_to(chip_ids, (LANES, rows)).T
    ids_out[...] = row_ids
    row_ids = jnp.concatenate([row_ids, row_ids], axis=1)
    txt_bf = unit_txt.astype(jnp.bfloat16)
    images = in_order(core, img[...], img2[...])
    term_out[...] = pair_term(
        factor, scalars[0], scalars[1], txt_bf, row_ids, images, chip_ids, (1, 0)
    )


def loss_kernel(
    factor, cols, scalars, place, far, far2, ids, unit, inverse, ids_in, term,
    dz_out, *rest,
):
    core, chip = place[0], place[1]
    *parts, straight, flipped = rest
    unit_txt = unit[...]
    txt_bf = unit_txt.astype(jnp.bfloat16)
    chip_ids = jnp.concatenate([ids[:1, :], ids[1:2, :]], axis=1)
    row_ids = jnp.concatenate([ids_in[...], ids_in[...]], axis=1)
    images = in_order(core, far[...], far2[...])
    scale = scalars[0]
    dvec = term[...] + pair_term(
        factor, scale, scalars[1], txt_bf, row_ids, images, chip_ids, (0, 1)
    )
    dvec = scale * dvec
    along = jnp.sum(unit_txt * dvec, axis=1, keepdims=True)
    dzed = ((dvec - unit_txt * along) * inverse[:, :1]).astype(jnp.bfloat16)
    straight[...] = dzed
    flipped[...] = dzed.T
    rows = dz_out.shape[0]
    dz_out[...] = straight[pl.ds(pl.multiple_of(core * rows, 16), rows), :]
    for k, part in enumerate(parts):
        start = pl.multiple_of((2 * (chip ^ k) + core) * cols, 16)
        part[...] = flipped[pl.ds(start, cols), :]


def packing(cols, depth):
    full, rest = divmod(depth, LANES)
    slots = 0
    if rest:
        slots = max(s for s in range(1, LANES // rest + 1) if cols % (16 * s) == 0)
    return full, rest, slots, cols * full + (cols // slots if slots else 0)


def product_kernel(chips, cols, depth, replica, place, *refs):
    grads, feats = refs[:chips], refs[chips : 3 * chips]
    outs = refs[3 * chips : 3 * chips + replica]
    feats_all, packed, sem = refs[3 * chips + replica :]
    core = place[0]
    rows = feats[0].shape[0]
    copies = []
    for i, (mine, theirs) in enumerate(zip(feats[:chips], feats[chips:])):
        for j, (block, slot) in enumerate(((mine, core), (theirs, 1 - core))):
            start = pl.multiple_of((2 * i + slot) * rows, rows)
            copies.append(
                pltpu.make_async_copy(
                    block, feats_all.at[pl.ds(start, rows), :], sem.at[2 * i + j]
                )
            )
    for copy in copies:
        copy.start()
    left = jnp.concatenate([g[...] for g in grads], axis=1)
    for copy in copies:
        copy.wait()
    full, rest, slots, _ = packing(cols, depth)
    local = jnp.dot(left, feats_all[...], preferred_element_type=jnp.float32)
    for r in range(replica):
        block = local[:, r * depth : (r + 1) * depth]
        for i in range(full):
            packed[r, i * cols : (i + 1) * cols, :] = block[:, i * LANES : (i + 1) * LANES]
        if slots:
            tall = cols // slots
            pieces = [block[s * tall : (s + 1) * tall, full * LANES :] for s in range(slots)]
            pieces.append(jnp.zeros((tall, LANES - slots * rest), jnp.float32))
            packed[r, full * cols :, :] = jnp.concatenate(pieces, axis=1)
    for k, out in enumerate(outs):
        out[...] = packed[place[2] ^ k].astype(out.dtype)


def final_kernel(cols, depth, *refs):
    out = refs[-1]
    total = refs[0][...].astype(jnp.float32)
    for ref in refs[1:-1]:
        total = total + ref[...].astype(jnp.float32)
    full, rest, slots, _ = packing(cols, depth)
    for i in range(full):
        out[:, i * LANES : (i + 1) * LANES] = total[i * cols : (i + 1) * cols, :]
    if slots:
        tall = cols // slots
        for s in range(slots):
            out[s * tall : (s + 1) * tall, full * LANES :] = total[
                full * cols :, s * rest : (s + 1) * rest
            ]


def box_shards(image_emb, text_feat, head_w, log_scale, bias, pair_ids):
    images = image_emb[0]
    feats = text_feat[0]
    rows, width = images.shape
    dp, replica = lax.axis_size("dp"), lax.axis_size("replica")
    chips = dp // 2
    cols, depth = width // dp, head_w.shape[0] // replica
    factor = LOSS_SCALE / (HOPS * rows)
    scalars = jnp.concatenate([jnp.exp(log_scale), bias])
    me, group = lax.axis_index("dp"), lax.axis_index("replica")
    place = jnp.stack([me & 1, me >> 1, group])

    def f32(*shape):
        return jax.ShapeDtypeStruct(shape, jnp.float32)

    def bf16(*shape):
        return jax.ShapeDtypeStruct(shape, jnp.bfloat16)

    far = rotated(images, "dp", -2)
    feats2 = swapped(feats, "dp", 1)
    images2 = swapped(images, "dp", 1)
    chip_ids = in_order(me & 1, pair_ids, swapped(pair_ids, "dp", 1))
    far_ids = rotated(jnp.tile(chip_ids, (1, 1)), "dp", -2)

    unit_txt, inverse, row_ids, own_term = pl.pallas_call(
        functools.partial(own_kernel, factor),
        out_shape=[
            f32(2 * rows, width),
            f32(2 * rows, LANES),
            jax.ShapeDtypeStruct((2 * rows, LANES), jnp.int32),
            f32(2 * rows, width),
        ],
        in_specs=[SMEM] * 2 + [VMEM] * 6,
        out_specs=[VMEM] * 4,
        compiler_params=grant(24),
        cost_estimate=pl.CostEstimate(flops=10000000000, bytes_accessed=1, transcendentals=0),
        name="own",
    )(scalars, place, feats, feats2, head_w, images, images2, chip_ids)

    feats_soon = after(feats, feats2)
    held = [swapped(feats_soon, "dp", 2 * k) for k in range(1, chips)]
    far2 = swapped(far, "dp", 1)

    dzed, *parts = pl.pallas_call(
        functools.partial(loss_kernel, factor, cols),
        out_shape=[bf16(rows, width)] + [bf16(cols, 2 * rows)] * chips,
        in_specs=[SMEM] * 2 + [VMEM] * 7,
        out_specs=[VMEM] * (1 + chips),
        scratch_shapes=[
            pltpu.VMEM((2 * rows, width), jnp.bfloat16),
            pltpu.VMEM((width, 2 * rows), jnp.bfloat16),
        ],
        compiler_params=grant(24),
        cost_estimate=pl.CostEstimate(flops=1, bytes_accessed=1, transcendentals=0),
        name="loss",
    )(scalars, place, far, far2, far_ids, unit_txt, inverse, row_ids, own_term)
    got = [swapped(parts[k], "dp", 2 * k) for k in range(1, chips)]
    held2 = [swapped(after(f, got[0]), "dp", 1) for f in held]
    grad_feat = lax.dot_general(dzed, head_w, NT, preferred_element_type=jnp.float32).astype(
        jnp.bfloat16
    )
    grad_feat, got = lax.optimization_barrier((grad_feat, got))

    tall = packing(cols, depth)[3]
    own, *pieces = pl.pallas_call(
        functools.partial(product_kernel, chips, cols, depth, replica),
        out_shape=[f32(tall, LANES)] + [bf16(tall, LANES)] * (replica - 1),
        in_specs=[SMEM] + [VMEM] * chips + [pl.BlockSpec(memory_space=pl.ANY)] * dp,
        out_specs=[VMEM] * replica,
        scratch_shapes=[
            pltpu.VMEM((dp * rows, head_w.shape[0]), jnp.bfloat16),
            pltpu.VMEM((replica, tall, LANES), jnp.float32),
            pltpu.SemaphoreType.DMA((dp,)),
        ],
        compiler_params=grant(24),
        cost_estimate=pl.CostEstimate(flops=1, bytes_accessed=1, transcendentals=0),
        name="product",
    )(place, parts[0], *got, feats, *held, feats2, *held2)
    order = sorted(range(1, replica), key=lambda k: (-(k & (replica // 2)), k))
    sums = [swapped(pieces[k - 1], "replica", k) for k in order]
    head_grad = pl.pallas_call(
        functools.partial(final_kernel, cols, depth),
        out_shape=f32(cols, depth),
        in_specs=[VMEM] * replica,
        out_specs=VMEM,
        compiler_params=grant(8),
        cost_estimate=pl.CostEstimate(flops=1, bytes_accessed=1, transcendentals=0),
        name="final",
    )(own, *sums)
    return (grad_feat[None], head_grad.T)


def general_shards(image_emb, text_feat, head_w, log_scale, bias, pair_ids):
    images = image_emb[0]
    feats = text_feat[0]
    ids = pair_ids[0]
    rows = feats.shape[0]
    dp = lax.axis_size("dp")
    replica = lax.axis_size("replica")
    chips = dp // 2
    factor = LOSS_SCALE / (HOPS * rows)
    scale = jnp.exp(log_scale[0])
    shift_b = bias[0]

    others = [rotated(images, "dp", -k) for k in range(1, HOPS)]
    other_ids = [rotated(ids, "dp", -k) for k in range(1, HOPS)]
    held = [feats] + [swapped(feats, "dp", 2 * k) for k in range(1, chips)]
    held2 = [swapped(f, "dp", 1) for f in held]

    raw = jnp.dot(feats, head_w, preferred_element_type=jnp.float32)
    norms = jnp.sqrt(jnp.sum(raw * raw, axis=1, keepdims=True) + 1e-06)
    unit_txt = raw / norms
    txt_bf = unit_txt.astype(jnp.bfloat16)

    imgs = jnp.concatenate([images] + others, axis=0)
    img_ids = jnp.concatenate([ids] + other_ids, axis=0)
    img32 = imgs.astype(jnp.float32)
    unit_img = (img32 / jnp.sqrt(jnp.sum(img32 * img32, axis=1, keepdims=True) + 1e-06)).astype(
        jnp.bfloat16
    )
    sims = lax.dot_general(
        txt_bf, unit_img, (((1,), (1,)), ((), ())), preferred_element_type=jnp.float32
    )
    match = (ids[:, None] == img_ids[None, :]).astype(jnp.float32)
    grads = (factor * (jax.nn.sigmoid(scale * sims + shift_b) - match)).astype(jnp.bfloat16)
    dvec = scale * jnp.dot(grads, unit_img, preferred_element_type=jnp.float32)
    dzed = ((dvec - unit_txt * jnp.sum(unit_txt * dvec, axis=1, keepdims=True)) / norms).astype(
        jnp.bfloat16
    )
    grad_feat = lax.dot_general(
        dzed, head_w, (((1,), (1,)), ((), ())), preferred_element_type=jnp.float32
    ).astype(jnp.bfloat16)

    me = lax.axis_index("dp")
    chip, core = me // 2, me % 2
    cols = head_w.shape[1] // dp
    dz_t = dzed.T
    parts = [
        lax.dynamic_slice_in_dim(dz_t, (chip ^ k) * 2 * cols, 2 * cols, 0) for k in range(chips)
    ]
    got = [parts[0]] + [swapped(parts[k], "dp", 2 * k) for k in range(1, chips)]
    got2 = [swapped(g, "dp", 1) for g in got]
    dz_all = jnp.concatenate(got + got2, axis=1)
    dz_all = lax.dynamic_slice_in_dim(dz_all, core * cols, cols, 0)
    feats_all = jnp.concatenate(held + held2, axis=0)
    local_head = lax.dot_general(
        feats_all, dz_all, (((0,), (1,)), ((), ())), preferred_element_type=jnp.float32
    )
    r = lax.axis_index("replica")
    depth = head_w.shape[0] // replica
    head_grad = lax.dynamic_slice_in_dim(local_head, r * depth, depth, 0)
    local_bf = local_head.astype(jnp.bfloat16)
    for k in range(1, replica):
        piece = lax.dynamic_slice_in_dim(local_bf, (r ^ k) * depth, depth, 0)
        head_grad = head_grad + swapped(piece, "replica", k).astype(jnp.float32)
    return (grad_feat[None], head_grad)


def shards(image_emb, text_feat, head_w, log_scale, bias, pair_ids):
    args = (image_emb, text_feat, head_w, log_scale, bias, pair_ids)
    dp, replica = lax.axis_size("dp"), lax.axis_size("replica")
    rows, width = image_emb.shape[1:]
    cols, depth = width // dp, head_w.shape[0] // replica
    if rows == LANES and cols % 16 == 0:
        return box_shards(*args)
    return general_shards(*args)


def solution(mesh):
    return jax.shard_map(
        shards,
        mesh=mesh,
        in_specs=(
            P("replica", "dp", None),
            P("replica", "dp", None),
            P(),
            P(),
            P(),
            P("replica", "dp"),
        ),
        out_specs=(P("replica", "dp", None), P("replica", "dp")),
        check_vma=False,
    )
```

```python
import functools

import jax
import jax.numpy as jnp
from jax import lax
from jax.experimental import pallas as pl
from jax.experimental.pallas import tpu as pltpu
from jax.sharding import PartitionSpec as P

HOPS = 3
LOSS_SCALE = 2048.0
LANES = 128
VMEM = pl.BlockSpec(memory_space=pltpu.VMEM)
SMEM = pl.BlockSpec(memory_space=pltpu.SMEM)
ANY = pl.BlockSpec(memory_space=pl.ANY)
NT = (((1,), (1,)), ((), ()))


def grant(mib):
    return pltpu.CompilerParams(vmem_limit_bytes=mib * 2**20)


def rotated(x, axis, by):
    size = lax.axis_size(axis)
    return lax.ppermute(x, axis, [(i, (i + by) % size) for i in range(size)])


def swapped(x, axis, mask):
    size = lax.axis_size(axis)
    return lax.ppermute(x, axis, [(i, i ^ mask) for i in range(size)])


def after(x, first):
    return lax.optimization_barrier((x, first))[0]


def unit_rows(images):
    wide = images.astype(jnp.float32)
    total = jnp.sum(wide * wide, axis=1, keepdims=True) + 1e-06
    return (wide * (1.0 / jnp.sqrt(total))).astype(jnp.bfloat16)


def pair_term(factor, log_scale, shift_b, txt_bf, row_ids, unit_img, image_ids, skip):
    scale = jnp.exp(jnp.full((1, txt_bf.shape[0]), log_scale, jnp.float32))
    sims = lax.dot_general(txt_bf, unit_img, NT, preferred_element_type=jnp.float32)
    rows = sims.shape[0] // 2
    match = (row_ids == image_ids).astype(jnp.float32)
    grads = factor * (jax.nn.sigmoid(scale * sims + shift_b) - match)
    row = lax.broadcasted_iota(jnp.int32, sims.shape, 0) >= rows
    col = lax.broadcasted_iota(jnp.int32, sims.shape, 1) >= rows
    away = (row.astype(jnp.int32) == skip) & (col.astype(jnp.int32) == 1 - skip)
    grads = jnp.where(away, 0.0, grads).astype(jnp.bfloat16)
    return jnp.dot(grads, unit_img, preferred_element_type=jnp.float32)


def own_kernel(
    factor, log_scale, bias, ids, ids2, raw, raw2, img, img2,
    unit_out, inverse_out, ids_out, term_out,
):
    core = lax.axis_index("dp") % 2
    text = jnp.concatenate([raw[...], raw2[...]], axis=0)
    rows = text.shape[0]
    chip_ids = jnp.concatenate([ids[...], ids2[...]], axis=1)
    row_ids = jnp.broadcast_to(chip_ids, (LANES, rows)).T
    ids_out[...] = row_ids
    row_ids = jnp.concatenate([row_ids, row_ids], axis=1)
    unit_img = unit_rows(jnp.concatenate([img[...], img2[...]], axis=0))
    inverse = 1.0 / jnp.sqrt(jnp.sum(text * text, axis=1, keepdims=True) + 1e-06)
    unit_txt = text * inverse
    unit_out[...] = unit_txt
    inverse_out[...] = jnp.broadcast_to(inverse, (rows, LANES))
    txt_bf = unit_txt.astype(jnp.bfloat16)
    term_out[...] = pair_term(
        factor, log_scale[0], bias[0], txt_bf, row_ids, unit_img, chip_ids, 1 - core
    )


def loss_kernel(
    factor, cols, log_scale, bias, far, far2, ids, ids2, unit, inverse, ids_in, term,
    dz_out, *rest,
):
    me = lax.axis_index("dp")
    core, chip = me % 2, me // 2
    *parts, flipped = rest
    unit_txt = unit[...]
    txt_bf = unit_txt.astype(jnp.bfloat16)
    chip_ids = jnp.concatenate([ids[...], ids2[...]], axis=1)
    row_ids = jnp.concatenate([ids_in[...], ids_in[...]], axis=1)
    unit_img = unit_rows(jnp.concatenate([far[...], far2[...]], axis=0))
    dvec = term[...] + pair_term(
        factor, log_scale[0], bias[0], txt_bf, row_ids, unit_img, chip_ids, core
    )
    scale = jnp.exp(jnp.full((1, dvec.shape[1]), log_scale[0], jnp.float32))
    dvec = scale * dvec
    along = jnp.sum(unit_txt * dvec, axis=1, keepdims=True)
    dzed = ((dvec - unit_txt * along) * inverse[:, :1]).astype(jnp.bfloat16)
    dz_out[...] = dzed[: dz_out.shape[0]]
    flipped[...] = dzed.T
    for k, part in enumerate(parts):
        start = pl.multiple_of((2 * (chip ^ k) + core) * cols, 16)
        part[...] = flipped[pl.ds(start, cols), :]


def packing(cols, depth):
    full, rest = divmod(depth, LANES)
    slots = 0
    if rest:
        slots = max(s for s in range(1, LANES // rest + 1) if cols % (16 * s) == 0)
    return full, rest, slots, cols * full + (cols // slots if slots else 0)


def gathered(blocks, held, sem):
    rows = blocks[0].shape[0]
    copies = [
        pltpu.make_async_copy(block, held.at[pl.ds(i * rows, rows), :], sem.at[i])
        for i, block in enumerate(blocks)
    ]
    for copy in copies:
        copy.start()
    return copies


def near_kernel(chips, *refs):
    grads, feats, (out, held, sem) = refs[:chips], refs[chips : 2 * chips + 1], refs[2 * chips + 1 :]
    copies = gathered(feats, held, sem)
    rows = feats[0].shape[0]
    left = [g[:, :rows] for g in grads] + [grads[0][:, rows:]]
    left = jnp.concatenate(left, axis=1)
    for copy in copies:
        copy.wait()
    out[...] = jnp.dot(left, held[...], preferred_element_type=jnp.float32)


def product_kernel(chips, cols, depth, replica, near, *refs):
    grads, feats = refs[: chips - 1], refs[chips - 1 : 2 * chips - 2]
    outs = refs[2 * chips - 2 : 2 * chips - 2 + replica]
    held, packed, sem = refs[2 * chips - 2 + replica :]
    copies = gathered(feats, held, sem)
    rows = feats[0].shape[0]
    left = jnp.concatenate([g[:, rows:] for g in grads], axis=1)
    for copy in copies:
        copy.wait()
    local = near[...] + jnp.dot(left, held[...], preferred_element_type=jnp.float32)
    full, rest, slots, _ = packing(cols, depth)
    for r in range(replica):
        block = local[:, r * depth : (r + 1) * depth]
        for i in range(full):
            packed[r, i * cols : (i + 1) * cols, :] = block[:, i * LANES : (i + 1) * LANES]
        if slots:
            tall = cols // slots
            pieces = [block[s * tall : (s + 1) * tall, full * LANES :] for s in range(slots)]
            pieces.append(jnp.zeros((tall, LANES - slots * rest), jnp.float32))
            packed[r, full * cols :, :] = jnp.concatenate(pieces, axis=1)
    for k, out in enumerate(outs):
        out[...] = packed[lax.axis_index("replica") ^ k].astype(out.dtype)


def final_kernel(cols, depth, *refs):
    out = refs[-1]
    total = refs[0][...].astype(jnp.float32)
    for ref in refs[1:-1]:
        total = total + ref[...].astype(jnp.float32)
    full, rest, slots, _ = packing(cols, depth)
    for i in range(full):
        out[:, i * LANES : (i + 1) * LANES] = total[i * cols : (i + 1) * cols, :]
    if slots:
        tall = cols // slots
        for s in range(slots):
            out[s * tall : (s + 1) * tall, full * LANES :] = total[
                full * cols :, s * rest : (s + 1) * rest
            ]


def box_shards(image_emb, text_feat, head_w, log_scale, bias, pair_ids):
    images = image_emb[0]
    feats = text_feat[0]
    rows, width = images.shape
    dp, replica = lax.axis_size("dp"), lax.axis_size("replica")
    chips = dp // 2
    cols, depth = width // dp, head_w.shape[0] // replica
    factor = LOSS_SCALE / (HOPS * rows)

    def f32(*shape):
        return jax.ShapeDtypeStruct(shape, jnp.float32)

    def bf16(*shape):
        return jax.ShapeDtypeStruct(shape, jnp.bfloat16)

    far = rotated(images, "dp", -2)
    far_ids = rotated(pair_ids, "dp", -2)
    feats2 = swapped(feats, "dp", 1)
    images2 = swapped(images, "dp", 1)
    pair_ids2 = swapped(pair_ids, "dp", 1)

    feats_in, feats2, images2, pair_ids2 = lax.optimization_barrier(
        (feats, feats2, images2, pair_ids2)
    )
    raw = jnp.dot(feats, head_w, preferred_element_type=jnp.float32)
    raw2 = jnp.dot(feats2, head_w, preferred_element_type=jnp.float32)
    unit_txt, inverse, row_ids, own_term = pl.pallas_call(
        functools.partial(own_kernel, factor),
        out_shape=[
            f32(2 * rows, width),
            f32(2 * rows, LANES),
            jax.ShapeDtypeStruct((2 * rows, LANES), jnp.int32),
            f32(2 * rows, width),
        ],
        in_specs=[SMEM] * 2 + [VMEM] * 6,
        out_specs=[VMEM] * 4,
        compiler_params=grant(24),
        cost_estimate=pl.CostEstimate(flops=10000000000, bytes_accessed=1, transcendentals=0),
        name="own",
    )(log_scale, bias, pair_ids, pair_ids2, raw, raw2, images, images2)

    feats_soon = feats
    held = [swapped(feats_soon, "dp", 2 * k) for k in range(1, chips)]
    far2 = swapped(after(far, (raw, raw2)), "dp", 1)
    far_ids2 = swapped(after(far_ids, far), "dp", 1)

    dzed, *parts = pl.pallas_call(
        functools.partial(loss_kernel, factor, cols),
        out_shape=[bf16(rows, width)] + [bf16(cols, 2 * rows)] * chips,
        in_specs=[SMEM] * 2 + [VMEM] * 8,
        out_specs=[VMEM] * (1 + chips),
        scratch_shapes=[pltpu.VMEM((width, 2 * rows), jnp.bfloat16)],
        compiler_params=grant(24),
        cost_estimate=pl.CostEstimate(flops=1, bytes_accessed=1, transcendentals=0),
        name="loss",
    )(log_scale, bias, far, far2, far_ids, far_ids2, unit_txt, inverse, row_ids, own_term)
    got = [swapped(parts[k], "dp", 2 * k) for k in range(1, chips)]
    grad_feat = lax.dot_general(dzed, head_w, NT, preferred_element_type=jnp.float32).astype(
        jnp.bfloat16
    )
    held2 = [swapped(after(f, grad_feat), "dp", 1) for f in held]

    near = pl.pallas_call(
        functools.partial(near_kernel, chips),
        out_shape=f32(cols, head_w.shape[0]),
        in_specs=[VMEM] * chips + [ANY] * (chips + 1),
        out_specs=VMEM,
        scratch_shapes=[
            pltpu.VMEM(((chips + 1) * rows, head_w.shape[0]), jnp.bfloat16),
            pltpu.SemaphoreType.DMA((chips + 1,)),
        ],
        compiler_params=grant(24),
        cost_estimate=pl.CostEstimate(flops=10000000000, bytes_accessed=1, transcendentals=0),
        name="near",
    )(parts[0], *got, feats, *held, feats2)
    tall = packing(cols, depth)[3]
    own, *pieces = pl.pallas_call(
        functools.partial(product_kernel, chips, cols, depth, replica),
        out_shape=[f32(tall, LANES)] + [bf16(tall, LANES)] * (replica - 1),
        in_specs=[VMEM] * chips + [ANY] * (chips - 1),
        out_specs=[VMEM] * replica,
        scratch_shapes=[
            pltpu.VMEM(((chips - 1) * rows, head_w.shape[0]), jnp.bfloat16),
            pltpu.VMEM((replica, tall, LANES), jnp.float32),
            pltpu.SemaphoreType.DMA((chips - 1,)),
        ],
        compiler_params=grant(24),
        cost_estimate=pl.CostEstimate(flops=1, bytes_accessed=1, transcendentals=0),
        name="product",
    )(near, *got, *held2)
    order = sorted(range(1, replica), key=lambda k: (-(k & (replica // 2)), k))
    sums = [swapped(pieces[k - 1], "replica", k) for k in order]
    head_grad = pl.pallas_call(
        functools.partial(final_kernel, cols, depth),
        out_shape=f32(cols, depth),
        in_specs=[VMEM] * replica,
        out_specs=VMEM,
        compiler_params=grant(8),
        cost_estimate=pl.CostEstimate(flops=1, bytes_accessed=1, transcendentals=0),
        name="final",
    )(own, *sums)
    return (grad_feat[None], head_grad.T)


def general_shards(image_emb, text_feat, head_w, log_scale, bias, pair_ids):
    images = image_emb[0]
    feats = text_feat[0]
    ids = pair_ids[0]
    rows = feats.shape[0]
    dp = lax.axis_size("dp")
    replica = lax.axis_size("replica")
    chips = dp // 2
    factor = LOSS_SCALE / (HOPS * rows)
    scale = jnp.exp(log_scale[0])
    shift_b = bias[0]

    others = [rotated(images, "dp", -k) for k in range(1, HOPS)]
    other_ids = [rotated(ids, "dp", -k) for k in range(1, HOPS)]
    held = [feats] + [swapped(feats, "dp", 2 * k) for k in range(1, chips)]
    held2 = [swapped(f, "dp", 1) for f in held]

    raw = jnp.dot(feats, head_w, preferred_element_type=jnp.float32)
    norms = jnp.sqrt(jnp.sum(raw * raw, axis=1, keepdims=True) + 1e-06)
    unit_txt = raw / norms
    txt_bf = unit_txt.astype(jnp.bfloat16)

    imgs = jnp.concatenate([images] + others, axis=0)
    img_ids = jnp.concatenate([ids] + other_ids, axis=0)
    img32 = imgs.astype(jnp.float32)
    unit_img = (img32 / jnp.sqrt(jnp.sum(img32 * img32, axis=1, keepdims=True) + 1e-06)).astype(
        jnp.bfloat16
    )
    sims = lax.dot_general(
        txt_bf, unit_img, (((1,), (1,)), ((), ())), preferred_element_type=jnp.float32
    )
    match = (ids[:, None] == img_ids[None, :]).astype(jnp.float32)
    grads = (factor * (jax.nn.sigmoid(scale * sims + shift_b) - match)).astype(jnp.bfloat16)
    dvec = scale * jnp.dot(grads, unit_img, preferred_element_type=jnp.float32)
    dzed = ((dvec - unit_txt * jnp.sum(unit_txt * dvec, axis=1, keepdims=True)) / norms).astype(
        jnp.bfloat16
    )
    grad_feat = lax.dot_general(
        dzed, head_w, (((1,), (1,)), ((), ())), preferred_element_type=jnp.float32
    ).astype(jnp.bfloat16)

    me = lax.axis_index("dp")
    chip, core = me // 2, me % 2
    cols = head_w.shape[1] // dp
    dz_t = dzed.T
    parts = [
        lax.dynamic_slice_in_dim(dz_t, (chip ^ k) * 2 * cols, 2 * cols, 0) for k in range(chips)
    ]
    got = [parts[0]] + [swapped(parts[k], "dp", 2 * k) for k in range(1, chips)]
    got2 = [swapped(g, "dp", 1) for g in got]
    dz_all = jnp.concatenate(got + got2, axis=1)
    dz_all = lax.dynamic_slice_in_dim(dz_all, core * cols, cols, 0)
    feats_all = jnp.concatenate(held + held2, axis=0)
    local_head = lax.dot_general(
        feats_all, dz_all, (((0,), (1,)), ((), ())), preferred_element_type=jnp.float32
    )
    r = lax.axis_index("replica")
    depth = head_w.shape[0] // replica
    head_grad = lax.dynamic_slice_in_dim(local_head, r * depth, depth, 0)
    local_bf = local_head.astype(jnp.bfloat16)
    for k in range(1, replica):
        piece = lax.dynamic_slice_in_dim(local_bf, (r ^ k) * depth, depth, 0)
        head_grad = head_grad + swapped(piece, "replica", k).astype(jnp.float32)
    return (grad_feat[None], head_grad)


def shards(image_emb, text_feat, head_w, log_scale, bias, pair_ids):
    args = (image_emb, text_feat, head_w, log_scale, bias, pair_ids)
    dp, replica = lax.axis_size("dp"), lax.axis_size("replica")
    rows, width = image_emb.shape[1:]
    cols, depth = width // dp, head_w.shape[0] // replica
    if rows == LANES and cols % 16 == 0:
        return box_shards(*args)
    return general_shards(*args)


def solution(mesh):
    return jax.shard_map(
        shards,
        mesh=mesh,
        in_specs=(
            P("replica", "dp", None),
            P("replica", "dp", None),
            P(),
            P(),
            P(),
            P("replica", "dp"),
        ),
        out_specs=(P("replica", "dp", None), P("replica", "dp")),
        check_vma=False,
    )
```

```python
import functools

import jax
import jax.numpy as jnp
from jax import lax
from jax.experimental import pallas as pl
from jax.experimental.pallas import tpu as pltpu
from jax.sharding import PartitionSpec as P

HOPS = 3
LOSS_SCALE = 2048.0
LANES = 128
VMEM = pl.BlockSpec(memory_space=pltpu.VMEM)
SMEM = pl.BlockSpec(memory_space=pltpu.SMEM)
ANY = pl.BlockSpec(memory_space=pl.ANY)
NT = (((1,), (1,)), ((), ()))


def grant(mib):
    return pltpu.CompilerParams(vmem_limit_bytes=mib * 2**20)


def rotated(x, axis, by):
    size = lax.axis_size(axis)
    return lax.ppermute(x, axis, [(i, (i + by) % size) for i in range(size)])


def swapped(x, axis, mask):
    size = lax.axis_size(axis)
    return lax.ppermute(x, axis, [(i, i ^ mask) for i in range(size)])


def after(x, first):
    return lax.optimization_barrier((x, first))[0]


def unit_rows(images):
    wide = images.astype(jnp.float32)
    total = jnp.sum(wide * wide, axis=1, keepdims=True) + 1e-06
    return (wide * (1.0 / jnp.sqrt(total))).astype(jnp.bfloat16)


def pair_term(factor, log_scale, shift_b, txt_bf, row_ids, unit_img, image_ids, skip):
    scale = jnp.exp(jnp.full((1, txt_bf.shape[0]), log_scale, jnp.float32))
    sims = lax.dot_general(txt_bf, unit_img, NT, preferred_element_type=jnp.float32)
    rows = sims.shape[0] // 2
    match = (row_ids == image_ids).astype(jnp.float32)
    grads = factor * (jax.nn.sigmoid(scale * sims + shift_b) - match)
    row = lax.broadcasted_iota(jnp.int32, sims.shape, 0) >= rows
    col = lax.broadcasted_iota(jnp.int32, sims.shape, 1) >= rows
    away = (row.astype(jnp.int32) == skip) & (col.astype(jnp.int32) == 1 - skip)
    grads = jnp.where(away, 0.0, grads).astype(jnp.bfloat16)
    return jnp.dot(grads, unit_img, preferred_element_type=jnp.float32)


def own_kernel(
    factor, log_scale, bias, ids, ids2, raw, raw2, img, img2,
    unit_out, inverse_out, ids_out, term_out,
):
    core = lax.axis_index("dp") % 2
    text = jnp.concatenate([raw[...], raw2[...]], axis=0)
    rows = text.shape[0]
    chip_ids = jnp.concatenate([ids[...], ids2[...]], axis=1)
    row_ids = jnp.broadcast_to(chip_ids, (LANES, rows)).T
    ids_out[...] = row_ids
    row_ids = jnp.concatenate([row_ids, row_ids], axis=1)
    unit_img = unit_rows(jnp.concatenate([img[...], img2[...]], axis=0))
    inverse = 1.0 / jnp.sqrt(jnp.sum(text * text, axis=1, keepdims=True) + 1e-06)
    unit_txt = text * inverse
    unit_out[...] = unit_txt
    inverse_out[...] = jnp.broadcast_to(inverse, (rows, LANES))
    txt_bf = unit_txt.astype(jnp.bfloat16)
    term_out[...] = pair_term(
        factor, log_scale[0], bias[0], txt_bf, row_ids, unit_img, chip_ids, 1 - core
    )


def loss_kernel(
    factor, cols, log_scale, bias, far, far2, ids, ids2, unit, inverse, ids_in, term,
    dz_out, *rest,
):
    me = lax.axis_index("dp")
    core, chip = me % 2, me // 2
    *parts, flipped = rest
    unit_txt = unit[...]
    txt_bf = unit_txt.astype(jnp.bfloat16)
    chip_ids = jnp.concatenate([ids[...], ids2[...]], axis=1)
    row_ids = jnp.concatenate([ids_in[...], ids_in[...]], axis=1)
    unit_img = unit_rows(jnp.concatenate([far[...], far2[...]], axis=0))
    dvec = term[...] + pair_term(
        factor, log_scale[0], bias[0], txt_bf, row_ids, unit_img, chip_ids, core
    )
    scale = jnp.exp(jnp.full((1, dvec.shape[1]), log_scale[0], jnp.float32))
    dvec = scale * dvec
    along = jnp.sum(unit_txt * dvec, axis=1, keepdims=True)
    dzed = ((dvec - unit_txt * along) * inverse[:, :1]).astype(jnp.bfloat16)
    dz_out[...] = dzed[: dz_out.shape[0]]
    flipped[...] = dzed.T
    for east, part in enumerate(parts):
        for north in range(2):
            start = pl.multiple_of((2 * (chip ^ east ^ (2 * north)) + core) * cols, 16)
            part[north * cols : (north + 1) * cols, :] = flipped[pl.ds(start, cols), :]


def packing(cols, depth):
    full, rest = divmod(depth, LANES)
    slots = 0
    if rest:
        slots = max(s for s in range(1, LANES // rest + 1) if cols % (16 * s) == 0)
    return full, rest, slots, cols * full + (cols // slots if slots else 0)


def gathered(blocks, held, sem):
    rows = blocks[0].shape[0]
    copies = [
        pltpu.make_async_copy(block, held.at[pl.ds(i * rows, rows), :], sem.at[i])
        for i, block in enumerate(blocks)
    ]
    for copy in copies:
        copy.start()
    return copies


def near_kernel(own, east, *refs):
    feats, (out, held, sem) = refs[:3], refs[3:]
    copies = gathered(feats, held, sem)
    left = jnp.concatenate([own[...], east[:, : feats[0].shape[0]]], axis=1)
    for copy in copies:
        copy.wait()
    out[...] = jnp.dot(left, held[...], preferred_element_type=jnp.float32)


def product_kernel(cols, depth, replica, near, east, feats, *refs):
    keeps, sends, packed = refs[:replica], refs[replica : 2 * replica - 1], refs[-1]
    local = near[...] + jnp.dot(
        east[:, feats.shape[0] :], feats[...], preferred_element_type=jnp.float32
    )
    full, rest, slots, tall = packing(cols, depth)
    for north in range(2):
        for r in range(replica):
            block = local[north * cols : (north + 1) * cols, r * depth : (r + 1) * depth]
            for i in range(full):
                packed[north, r, i * cols : (i + 1) * cols, :] = block[:, i * LANES : (i + 1) * LANES]
            if slots:
                high = cols // slots
                pieces = [block[s * high : (s + 1) * high, full * LANES :] for s in range(slots)]
                pieces.append(jnp.zeros((high, LANES - slots * rest), jnp.float32))
                packed[north, r, full * cols :, :] = jnp.concatenate(pieces, axis=1)
    me = lax.axis_index("replica")
    for k, out in enumerate(keeps):
        out[...] = packed[0, me ^ k]
    for k in range(2, replica):
        sends[k - 1][...] = packed[1, me ^ k].astype(jnp.bfloat16)
    for k in range(2):
        sends[0][k * tall : (k + 1) * tall, :] = packed[1, me ^ k].astype(jnp.bfloat16)


def final_kernel(cols, depth, *refs):
    out = refs[-1]
    total = refs[0][...].astype(jnp.float32)
    for ref in refs[1:-1]:
        total = total + ref[...].astype(jnp.float32)
    full, rest, slots, _ = packing(cols, depth)
    for i in range(full):
        out[:, i * LANES : (i + 1) * LANES] = total[i * cols : (i + 1) * cols, :]
    if slots:
        tall = cols // slots
        for s in range(slots):
            out[s * tall : (s + 1) * tall, full * LANES :] = total[
                full * cols :, s * rest : (s + 1) * rest
            ]


def box_shards(image_emb, text_feat, head_w, log_scale, bias, pair_ids):
    images = image_emb[0]
    feats = text_feat[0]
    rows, width = images.shape
    dp, replica = lax.axis_size("dp"), lax.axis_size("replica")
    chips = dp // 2
    cols, depth = width // dp, head_w.shape[0] // replica
    factor = LOSS_SCALE / (HOPS * rows)

    def f32(*shape):
        return jax.ShapeDtypeStruct(shape, jnp.float32)

    def bf16(*shape):
        return jax.ShapeDtypeStruct(shape, jnp.bfloat16)

    far = rotated(images, "dp", -2)
    far_ids = rotated(pair_ids, "dp", -2)
    feats2 = swapped(feats, "dp", 1)
    images2 = swapped(images, "dp", 1)
    pair_ids2 = swapped(pair_ids, "dp", 1)

    feats_in, feats2, images2, pair_ids2 = lax.optimization_barrier(
        (feats, feats2, images2, pair_ids2)
    )
    raw = jnp.dot(feats, head_w, preferred_element_type=jnp.float32)
    raw2 = jnp.dot(feats2, head_w, preferred_element_type=jnp.float32)
    unit_txt, inverse, row_ids, own_term = pl.pallas_call(
        functools.partial(own_kernel, factor),
        out_shape=[
            f32(2 * rows, width),
            f32(2 * rows, LANES),
            jax.ShapeDtypeStruct((2 * rows, LANES), jnp.int32),
            f32(2 * rows, width),
        ],
        in_specs=[SMEM] * 2 + [VMEM] * 6,
        out_specs=[VMEM] * 4,
        compiler_params=grant(24),
        cost_estimate=pl.CostEstimate(flops=10000000000, bytes_accessed=1, transcendentals=0),
        name="own",
    )(log_scale, bias, pair_ids, pair_ids2, raw, raw2, images, images2)

    feats_soon = feats
    east_feats = swapped(feats_soon, "dp", 2)
    far2 = swapped(after(far, (raw, raw2)), "dp", 1)
    far_ids2 = swapped(after(far_ids, far), "dp", 1)

    dzed, same, other = pl.pallas_call(
        functools.partial(loss_kernel, factor, cols),
        out_shape=[bf16(rows, width)] + [bf16(2 * cols, 2 * rows)] * 2,
        in_specs=[SMEM] * 2 + [VMEM] * 8,
        out_specs=[VMEM] * 3,
        scratch_shapes=[pltpu.VMEM((width, 2 * rows), jnp.bfloat16)],
        compiler_params=grant(24),
        cost_estimate=pl.CostEstimate(flops=5000000000, bytes_accessed=1, transcendentals=0),
        name="loss",
    )(log_scale, bias, far, far2, far_ids, far_ids2, unit_txt, inverse, row_ids, own_term)
    east = swapped(other, "dp", 2)
    grad_feat = lax.dot_general(dzed, head_w, NT, preferred_element_type=jnp.float32).astype(
        jnp.bfloat16
    )
    east_feats2 = swapped(after(east_feats, same), "dp", 1)
    tall = packing(cols, depth)[3]
    near = pl.pallas_call(
        near_kernel,
        out_shape=f32(2 * cols, head_w.shape[0]),
        in_specs=[VMEM] * 2 + [ANY] * 3,
        out_specs=VMEM,
        scratch_shapes=[
            pltpu.VMEM((3 * rows, head_w.shape[0]), jnp.bfloat16),
            pltpu.SemaphoreType.DMA((3,)),
        ],
        compiler_params=grant(24),
        cost_estimate=pl.CostEstimate(flops=10000000000, bytes_accessed=1, transcendentals=0),
        name="near",
    )(same, east, feats, feats2, east_feats)
    products = pl.pallas_call(
        functools.partial(product_kernel, cols, depth, replica),
        out_shape=[f32(tall, LANES)] * replica
        + [bf16(2 * tall, LANES)]
        + [bf16(tall, LANES)] * (replica - 2),
        in_specs=[VMEM] * 3,
        out_specs=[VMEM] * (2 * replica - 1),
        scratch_shapes=[pltpu.VMEM((2, replica, tall, LANES), jnp.float32)],
        compiler_params=grant(24),
        cost_estimate=pl.CostEstimate(flops=1, bytes_accessed=1, transcendentals=0),
        name="product",
    )(near, east, east_feats2)
    keeps, sends = products[:replica], products[replica:]
    sums = []
    for k in range(2, replica):
        total = keeps[k] + swapped(sends[k - 1], "dp", 4).astype(jnp.float32)
        sums.append(swapped(total.astype(jnp.bfloat16), "replica", k))
    last = swapped(sends[0], "dp", 4).astype(jnp.float32)
    total = keeps[1] + last[tall:]
    sums.append(swapped(total.astype(jnp.bfloat16), "replica", 1))
    own = keeps[0] + last[:tall]
    head_grad = pl.pallas_call(
        functools.partial(final_kernel, cols, depth),
        out_shape=f32(cols, depth),
        in_specs=[VMEM] * replica,
        out_specs=VMEM,
        compiler_params=grant(8),
        cost_estimate=pl.CostEstimate(flops=1, bytes_accessed=1, transcendentals=0),
        name="final",
    )(own, *sums)
    return (grad_feat[None], head_grad.T)


def general_shards(image_emb, text_feat, head_w, log_scale, bias, pair_ids):
    images = image_emb[0]
    feats = text_feat[0]
    ids = pair_ids[0]
    rows = feats.shape[0]
    dp = lax.axis_size("dp")
    replica = lax.axis_size("replica")
    chips = dp // 2
    factor = LOSS_SCALE / (HOPS * rows)
    scale = jnp.exp(log_scale[0])
    shift_b = bias[0]

    others = [rotated(images, "dp", -k) for k in range(1, HOPS)]
    other_ids = [rotated(ids, "dp", -k) for k in range(1, HOPS)]
    held = [feats] + [swapped(feats, "dp", 2 * k) for k in range(1, chips)]
    held2 = [swapped(f, "dp", 1) for f in held]

    raw = jnp.dot(feats, head_w, preferred_element_type=jnp.float32)
    norms = jnp.sqrt(jnp.sum(raw * raw, axis=1, keepdims=True) + 1e-06)
    unit_txt = raw / norms
    txt_bf = unit_txt.astype(jnp.bfloat16)

    imgs = jnp.concatenate([images] + others, axis=0)
    img_ids = jnp.concatenate([ids] + other_ids, axis=0)
    img32 = imgs.astype(jnp.float32)
    unit_img = (img32 / jnp.sqrt(jnp.sum(img32 * img32, axis=1, keepdims=True) + 1e-06)).astype(
        jnp.bfloat16
    )
    sims = lax.dot_general(
        txt_bf, unit_img, (((1,), (1,)), ((), ())), preferred_element_type=jnp.float32
    )
    match = (ids[:, None] == img_ids[None, :]).astype(jnp.float32)
    grads = (factor * (jax.nn.sigmoid(scale * sims + shift_b) - match)).astype(jnp.bfloat16)
    dvec = scale * jnp.dot(grads, unit_img, preferred_element_type=jnp.float32)
    dzed = ((dvec - unit_txt * jnp.sum(unit_txt * dvec, axis=1, keepdims=True)) / norms).astype(
        jnp.bfloat16
    )
    grad_feat = lax.dot_general(
        dzed, head_w, (((1,), (1,)), ((), ())), preferred_element_type=jnp.float32
    ).astype(jnp.bfloat16)

    me = lax.axis_index("dp")
    chip, core = me // 2, me % 2
    cols = head_w.shape[1] // dp
    dz_t = dzed.T
    parts = [
        lax.dynamic_slice_in_dim(dz_t, (chip ^ k) * 2 * cols, 2 * cols, 0) for k in range(chips)
    ]
    got = [parts[0]] + [swapped(parts[k], "dp", 2 * k) for k in range(1, chips)]
    got2 = [swapped(g, "dp", 1) for g in got]
    dz_all = jnp.concatenate(got + got2, axis=1)
    dz_all = lax.dynamic_slice_in_dim(dz_all, core * cols, cols, 0)
    feats_all = jnp.concatenate(held + held2, axis=0)
    local_head = lax.dot_general(
        feats_all, dz_all, (((0,), (1,)), ((), ())), preferred_element_type=jnp.float32
    )
    r = lax.axis_index("replica")
    depth = head_w.shape[0] // replica
    head_grad = lax.dynamic_slice_in_dim(local_head, r * depth, depth, 0)
    local_bf = local_head.astype(jnp.bfloat16)
    for k in range(1, replica):
        piece = lax.dynamic_slice_in_dim(local_bf, (r ^ k) * depth, depth, 0)
        head_grad = head_grad + swapped(piece, "replica", k).astype(jnp.float32)
    return (grad_feat[None], head_grad)


def shards(image_emb, text_feat, head_w, log_scale, bias, pair_ids):
    args = (image_emb, text_feat, head_w, log_scale, bias, pair_ids)
    dp, replica = lax.axis_size("dp"), lax.axis_size("replica")
    rows, width = image_emb.shape[1:]
    cols, depth = width // dp, head_w.shape[0] // replica
    if dp == 8 and replica == 4 and rows == LANES and cols % 16 == 0:
        return box_shards(*args)
    return general_shards(*args)


def solution(mesh):
    return jax.shard_map(
        shards,
        mesh=mesh,
        in_specs=(
            P("replica", "dp", None),
            P("replica", "dp", None),
            P(),
            P(),
            P(),
            P("replica", "dp"),
        ),
        out_specs=(P("replica", "dp", None), P("replica", "dp")),
        check_vma=False,
    )
```

```python
import functools

import jax
import jax.numpy as jnp
from jax import lax
from jax.experimental import pallas as pl
from jax.experimental.pallas import tpu as pltpu
from jax.sharding import PartitionSpec as P

HOPS = 3
LOSS_SCALE = 2048.0
LANES = 128
GATHER, REDUCE = (1, 2)
LONG = pl.CostEstimate(flops=10**10, bytes_accessed=1, transcendentals=0)
VMEM = pl.BlockSpec(memory_space=pltpu.VMEM)
SMEM = pl.BlockSpec(memory_space=pltpu.SMEM)
NT = (((1,), (1,)), ((), ()))


def grant(mib):
    return pltpu.CompilerParams(vmem_limit_bytes=mib * 2**20)


def rotated(x, axis, by):
    size = lax.axis_size(axis)
    return lax.ppermute(x, axis, [(i, (i + by) % size) for i in range(size)])


def swapped(x, axis, mask):
    size = lax.axis_size(axis)
    return lax.ppermute(x, axis, [(i, i ^ mask) for i in range(size)])


def after(x, first):
    return lax.optimization_barrier((x, first))[0]


def unit_rows(images):
    wide = images.astype(jnp.float32)
    total = jnp.sum(wide * wide, axis=1, keepdims=True) + 1e-06
    return (wide * (1.0 / jnp.sqrt(total))).astype(jnp.bfloat16)


def pair_term(factor, log_scale, shift_b, txt_bf, row_ids, unit_img, image_ids, skip):
    scale = jnp.exp(jnp.full((1, txt_bf.shape[0]), log_scale, jnp.float32))
    sims = lax.dot_general(txt_bf, unit_img, NT, preferred_element_type=jnp.float32)
    rows = sims.shape[0] // 2
    match = (row_ids == image_ids).astype(jnp.float32)
    grads = factor * (jax.nn.sigmoid(scale * sims + shift_b) - match)
    row = lax.broadcasted_iota(jnp.int32, sims.shape, 0) >= rows
    col = lax.broadcasted_iota(jnp.int32, sims.shape, 1) >= rows
    away = (row.astype(jnp.int32) == skip) & (col.astype(jnp.int32) == 1 - skip)
    grads = jnp.where(away, 0.0, grads).astype(jnp.bfloat16)
    return jnp.dot(grads, unit_img, preferred_element_type=jnp.float32)


def own_kernel(
    factor, log_scale, bias, ids, ids2, raw, raw2, img, img2,
    unit_out, inverse_out, ids_out, term_out,
):
    core = lax.axis_index("dp") % 2
    text = jnp.concatenate([raw[...], raw2[...]], axis=0)
    rows = text.shape[0]
    chip_ids = jnp.concatenate([ids[...], ids2[...]], axis=1)
    row_ids = jnp.broadcast_to(chip_ids, (LANES, rows)).T
    ids_out[...] = row_ids
    row_ids = jnp.concatenate([row_ids, row_ids], axis=1)
    unit_img = unit_rows(jnp.concatenate([img[...], img2[...]], axis=0))
    inverse = 1.0 / jnp.sqrt(jnp.sum(text * text, axis=1, keepdims=True) + 1e-06)
    unit_txt = text * inverse
    unit_out[...] = unit_txt
    inverse_out[...] = jnp.broadcast_to(inverse, (rows, LANES))
    txt_bf = unit_txt.astype(jnp.bfloat16)
    term_out[...] = pair_term(
        factor, log_scale[0], bias[0], txt_bf, row_ids, unit_img, chip_ids, 1 - core
    )


def loss_kernel(
    factor, cols, log_scale, bias, far, far2, ids, ids2, unit, inverse, ids_in, term,
    dz_out, *rest,
):
    me = lax.axis_index("dp")
    core, chip = me % 2, me // 2
    *parts, flipped = rest
    unit_txt = unit[...]
    txt_bf = unit_txt.astype(jnp.bfloat16)
    chip_ids = jnp.concatenate([ids[...], ids2[...]], axis=1)
    row_ids = jnp.concatenate([ids_in[...], ids_in[...]], axis=1)
    unit_img = unit_rows(jnp.concatenate([far[...], far2[...]], axis=0))
    dvec = term[...] + pair_term(
        factor, log_scale[0], bias[0], txt_bf, row_ids, unit_img, chip_ids, core
    )
    scale = jnp.exp(jnp.full((1, dvec.shape[1]), log_scale[0], jnp.float32))
    dvec = scale * dvec
    along = jnp.sum(unit_txt * dvec, axis=1, keepdims=True)
    dzed = ((dvec - unit_txt * along) * inverse[:, :1]).astype(jnp.bfloat16)
    dz_out[...] = dzed[: dz_out.shape[0]]
    flipped[...] = dzed.T
    for east, part in enumerate(parts):
        for north in range(2):
            start = pl.multiple_of((2 * (chip ^ (GATHER * east) ^ (REDUCE * north)) + core) * cols, 16)
            part[north * cols : (north + 1) * cols, :] = flipped[pl.ds(start, cols), :]


def packing(cols, depth):
    full, rest = divmod(depth, LANES)
    slots = 0
    if rest:
        slots = max(s for s in range(1, LANES // rest + 1) if cols % (16 * s) == 0)
    return full, rest, slots, cols * full + (cols // slots if slots else 0)


def early_kernel(own, feats, feats2, out):
    rows = feats.shape[0]
    out[...] = jnp.dot(
        own[:, :rows], feats[...], preferred_element_type=jnp.float32
    ) + jnp.dot(own[:, rows:], feats2[...], preferred_element_type=jnp.float32)


def near_kernel(early, east, feats, out):
    out[...] = early[...] + jnp.dot(
        east[:, : feats.shape[0]], feats[...], preferred_element_type=jnp.float32
    )


def product_kernel(cols, depth, replica, near, east, feats, *refs):
    keeps, sends, packed = refs[:replica], refs[replica : 2 * replica], refs[-1]
    local = near[...] + jnp.dot(
        east[:, feats.shape[0] :], feats[...], preferred_element_type=jnp.float32
    )
    full, rest, slots, tall = packing(cols, depth)
    for north in range(2):
        for r in range(replica):
            block = local[north * cols : (north + 1) * cols, r * depth : (r + 1) * depth]
            for i in range(full):
                packed[north, r, i * cols : (i + 1) * cols, :] = block[:, i * LANES : (i + 1) * LANES]
            if slots:
                high = cols // slots
                pieces = [block[s * high : (s + 1) * high, full * LANES :] for s in range(slots)]
                pieces.append(jnp.zeros((high, LANES - slots * rest), jnp.float32))
                packed[north, r, full * cols :, :] = jnp.concatenate(pieces, axis=1)
    me = lax.axis_index("replica")
    for k, out in enumerate(keeps):
        out[...] = packed[0, me ^ k]
    for k, out in enumerate(sends):
        out[...] = packed[1, me ^ k].astype(jnp.bfloat16)


def final_kernel(cols, depth, *refs):
    out = refs[-1]
    total = refs[0][...].astype(jnp.float32)
    for ref in refs[1:-1]:
        total = total + ref[...].astype(jnp.float32)
    full, rest, slots, _ = packing(cols, depth)
    for i in range(full):
        out[:, i * LANES : (i + 1) * LANES] = total[i * cols : (i + 1) * cols, :]
    if slots:
        tall = cols // slots
        for s in range(slots):
            out[s * tall : (s + 1) * tall, full * LANES :] = total[
                full * cols :, s * rest : (s + 1) * rest
            ]


def box_shards(image_emb, text_feat, head_w, log_scale, bias, pair_ids):
    images = image_emb[0]
    feats = text_feat[0]
    rows, width = images.shape
    dp, replica = lax.axis_size("dp"), lax.axis_size("replica")
    chips = dp // 2
    cols, depth = width // dp, head_w.shape[0] // replica
    factor = LOSS_SCALE / (HOPS * rows)

    def f32(*shape):
        return jax.ShapeDtypeStruct(shape, jnp.float32)

    def bf16(*shape):
        return jax.ShapeDtypeStruct(shape, jnp.bfloat16)

    far = rotated(images, "dp", -2)
    far_ids = rotated(pair_ids, "dp", -2)
    pair_ids2 = swapped(pair_ids, "dp", 1)
    feats2 = swapped(feats, "dp", 1)
    images2 = swapped(images, "dp", 1)

    feats_in, feats2, images2, pair_ids2 = lax.optimization_barrier(
        (feats, feats2, images2, pair_ids2)
    )
    raw = jnp.dot(feats, head_w, preferred_element_type=jnp.float32)
    raw2 = jnp.dot(feats2, head_w, preferred_element_type=jnp.float32)
    unit_txt, inverse, row_ids, own_term = pl.pallas_call(
        functools.partial(own_kernel, factor),
        out_shape=[
            f32(2 * rows, width),
            f32(2 * rows, LANES),
            jax.ShapeDtypeStruct((2 * rows, LANES), jnp.int32),
            f32(2 * rows, width),
        ],
        in_specs=[SMEM] * 2 + [VMEM] * 6,
        out_specs=[VMEM] * 4,
        compiler_params=grant(24),
        cost_estimate=LONG,
        name="own",
    )(log_scale, bias, pair_ids, pair_ids2, raw, raw2, images, images2)

    feats_soon = feats
    east_feats = swapped(feats_soon, "dp", 2 * GATHER)
    far2 = swapped(after(far, (raw, raw2)), "dp", 1)
    far_ids2 = swapped(after(far_ids, far), "dp", 1)

    dzed, same, other = pl.pallas_call(
        functools.partial(loss_kernel, factor, cols),
        out_shape=[bf16(rows, width)] + [bf16(2 * cols, 2 * rows)] * 2,
        in_specs=[SMEM] * 2 + [VMEM] * 8,
        out_specs=[VMEM] * 3,
        scratch_shapes=[pltpu.VMEM((width, 2 * rows), jnp.bfloat16)],
        compiler_params=grant(24),
        name="loss",
    )(log_scale, bias, far, far2, far_ids, far_ids2, unit_txt, inverse, row_ids, own_term)
    east = swapped(other, "dp", 2 * GATHER)
    grad_feat = lax.dot_general(dzed, head_w, NT, preferred_element_type=jnp.float32).astype(
        jnp.bfloat16
    )
    east_feats2 = swapped(after(east_feats, grad_feat), "dp", 1)
    tall = packing(cols, depth)[3]
    early = pl.pallas_call(
        early_kernel,
        out_shape=f32(2 * cols, head_w.shape[0]),
        in_specs=[VMEM] * 3,
        out_specs=VMEM,
        compiler_params=grant(24),
        name="early",
    )(same, feats, feats2)
    near = pl.pallas_call(
        near_kernel,
        out_shape=f32(2 * cols, head_w.shape[0]),
        in_specs=[VMEM] * 3,
        out_specs=VMEM,
        compiler_params=grant(24),
        cost_estimate=LONG,
        name="near",
    )(early, east, east_feats)
    products = pl.pallas_call(
        functools.partial(product_kernel, cols, depth, replica),
        out_shape=[f32(tall, LANES)] * replica + [bf16(tall, LANES)] * replica,
        in_specs=[VMEM] * 3,
        out_specs=[VMEM] * (2 * replica),
        scratch_shapes=[pltpu.VMEM((2, replica, tall, LANES), jnp.float32)],
        compiler_params=grant(24),
        name="product",
    )(near, east, east_feats2)
    keeps, sends = products[:replica], products[replica:]
    got = {}
    for k in (1, 2, 3, 0):
        got[k] = swapped(after(sends[k], got[{}[k]]) if k in {} else sends[k], "dp", 2 * REDUCE)
    sums = []
    for k in (1, 3, 2):
        total = keeps[k] + got[k].astype(jnp.float32)
        sums.append(swapped(total.astype(jnp.bfloat16), "replica", k))
    head_grad = pl.pallas_call(
        functools.partial(final_kernel, cols, depth),
        out_shape=f32(cols, depth),
        in_specs=[VMEM] * (replica + 1),
        out_specs=VMEM,
        compiler_params=grant(8),
        name="final",
    )(keeps[0], got[0], *sums)
    return (grad_feat[None], head_grad.T)


def general_shards(image_emb, text_feat, head_w, log_scale, bias, pair_ids):
    images = image_emb[0]
    feats = text_feat[0]
    ids = pair_ids[0]
    rows = feats.shape[0]
    dp = lax.axis_size("dp")
    replica = lax.axis_size("replica")
    chips = dp // 2
    factor = LOSS_SCALE / (HOPS * rows)
    scale = jnp.exp(log_scale[0])
    shift_b = bias[0]

    others = [rotated(images, "dp", -k) for k in range(1, HOPS)]
    other_ids = [rotated(ids, "dp", -k) for k in range(1, HOPS)]
    held = [feats] + [swapped(feats, "dp", 2 * k) for k in range(1, chips)]
    held2 = [swapped(f, "dp", 1) for f in held]

    raw = jnp.dot(feats, head_w, preferred_element_type=jnp.float32)
    norms = jnp.sqrt(jnp.sum(raw * raw, axis=1, keepdims=True) + 1e-06)
    unit_txt = raw / norms
    txt_bf = unit_txt.astype(jnp.bfloat16)

    imgs = jnp.concatenate([images] + others, axis=0)
    img_ids = jnp.concatenate([ids] + other_ids, axis=0)
    img32 = imgs.astype(jnp.float32)
    unit_img = (img32 / jnp.sqrt(jnp.sum(img32 * img32, axis=1, keepdims=True) + 1e-06)).astype(
        jnp.bfloat16
    )
    sims = lax.dot_general(
        txt_bf, unit_img, (((1,), (1,)), ((), ())), preferred_element_type=jnp.float32
    )
    match = (ids[:, None] == img_ids[None, :]).astype(jnp.float32)
    grads = (factor * (jax.nn.sigmoid(scale * sims + shift_b) - match)).astype(jnp.bfloat16)
    dvec = scale * jnp.dot(grads, unit_img, preferred_element_type=jnp.float32)
    dzed = ((dvec - unit_txt * jnp.sum(unit_txt * dvec, axis=1, keepdims=True)) / norms).astype(
        jnp.bfloat16
    )
    grad_feat = lax.dot_general(
        dzed, head_w, (((1,), (1,)), ((), ())), preferred_element_type=jnp.float32
    ).astype(jnp.bfloat16)

    me = lax.axis_index("dp")
    chip, core = me // 2, me % 2
    cols = head_w.shape[1] // dp
    dz_t = dzed.T
    parts = [
        lax.dynamic_slice_in_dim(dz_t, (chip ^ k) * 2 * cols, 2 * cols, 0) for k in range(chips)
    ]
    got = [parts[0]] + [swapped(parts[k], "dp", 2 * k) for k in range(1, chips)]
    got2 = [swapped(g, "dp", 1) for g in got]
    dz_all = jnp.concatenate(got + got2, axis=1)
    dz_all = lax.dynamic_slice_in_dim(dz_all, core * cols, cols, 0)
    feats_all = jnp.concatenate(held + held2, axis=0)
    local_head = lax.dot_general(
        feats_all, dz_all, (((0,), (1,)), ((), ())), preferred_element_type=jnp.float32
    )
    r = lax.axis_index("replica")
    depth = head_w.shape[0] // replica
    head_grad = lax.dynamic_slice_in_dim(local_head, r * depth, depth, 0)
    local_bf = local_head.astype(jnp.bfloat16)
    for k in range(1, replica):
        piece = lax.dynamic_slice_in_dim(local_bf, (r ^ k) * depth, depth, 0)
        head_grad = head_grad + swapped(piece, "replica", k).astype(jnp.float32)
    return (grad_feat[None], head_grad)


def shards(image_emb, text_feat, head_w, log_scale, bias, pair_ids):
    args = (image_emb, text_feat, head_w, log_scale, bias, pair_ids)
    dp, replica = lax.axis_size("dp"), lax.axis_size("replica")
    rows, width = image_emb.shape[1:]
    cols, depth = width // dp, head_w.shape[0] // replica
    if dp == 8 and replica == 4 and rows == LANES and cols % 16 == 0:
        return box_shards(*args)
    return general_shards(*args)


def solution(mesh):
    return jax.shard_map(
        shards,
        mesh=mesh,
        in_specs=(
            P("replica", "dp", None),
            P("replica", "dp", None),
            P(),
            P(),
            P(),
            P("replica", "dp"),
        ),
        out_specs=(P("replica", "dp", None), P("replica", "dp")),
        check_vma=False,
    )
```
